32 devices in a mesh: row: 8 (over y, x, core), col: 4 (over z).
Axes of the slice: x: 2, y: 2, z: 4, core: 2. Of those that a mesh axis runs over, the one named last changes fastest.
Arguments:
- embeddings: bfloat16 [4096, 256], P(('row', 'col')), may hold values from -6 to 6
- cotangent: bfloat16 [4096, 256], P(('row', 'col')), may hold values from -6 to 6
- weight: bfloat16 [256, 256], replicated, may hold values from -0.375 to 0.375
- tiles: bfloat16 [32, 128, 128, 128], P(('row', 'col')), may hold values from -0.078125 to 0.078125
- tile_dst: int32 [32, 128], P(('row', 'col')), may hold values from 0 to 3
- tile_src: int32 [32, 128], P(('row', 'col')), may hold values from 0 to 7
- tile_count: int32 [32], P(('row', 'col')), may hold values from 1 to 128, as said below
Outputs:
- output: bfloat16 [4096, 256], P(('row', 'col'))
- grad_embeddings: bfloat16 [4096, 256], P(('row', 'col'))
- grad_weight: float32 [256, 256], replicated
The draws below stay inside these ranges and needn't reach their ends.
Inputs may be any that keep to these rules, and one draw needn't show every extreme that they name: `tile_count`: at least one device has exactly 128 live slots.
All inputs are finite; a program needn't handle non-finite values.
Results may differ from the reference program's by a relative error of at most 0.012.
Values may be sent and summed in bfloat16 or wider, within the bound.
A program may use at most 128 MiB of HBM per device.

```python
import math
import jax
import jax.numpy as jnp
from jax import lax

D = 256
BLOCK = 128
TILES_MAX = 128
DEVICES_ALL = 32
USERS = 4096
N_ROW = 8
N_COL = 4
DEVICES = 32


def draw_tile_count(key, part):
    first_key, second_key = jax.random.split(key)
    uniform_ints = jax.random.randint(first_key, (DEVICES,), 1, TILES_MAX + 1, dtype=jnp.int32)
    counts = jnp.maximum(uniform_ints * uniform_ints // TILES_MAX, 1)
    busiest = jax.random.randint(second_key, (), 0, DEVICES, dtype=jnp.int32)
    counts = counts.at[busiest].set(TILES_MAX)
    return counts.astype(jnp.int32)


def with_ends(result, key, least, largest):
    place = [jax.random.randint(jax.random.fold_in(key, axis), (), 0, length) for axis, length in enumerate(result.shape)]
    widest = result.shape.index(max(result.shape))
    beside = place[:widest] + [(place[widest] + 1) % result.shape[widest]] + place[widest + 1:]
    return result.at[tuple(place)].set(least).at[tuple(beside)].set(largest)


def block_levels(key, shape, cuts, smallest, largest):
    gain, own = 1.0, jax.random.fold_in(key, 6)
    for dim, shards_of in cuts:
        draws = jnp.exp(jax.random.uniform(jax.random.fold_in(own, dim), (shards_of,), jnp.float32, smallest / len(cuts), largest / len(cuts)))
        gain = gain * jnp.repeat(draws, shape[dim] // shards_of).reshape([-1 if axis == dim else 1 for axis in range(len(shape))])
    return gain


def normal_values(stream_key, shape, scale, bound, cuts=(), kind=jnp.bfloat16):
    loudness = block_levels(stream_key, shape, cuts, -0.22, 0.18) if cuts else 1.0
    drawn = jax.random.normal(stream_key, shape, jnp.float32) * scale * loudness
    return jnp.minimum(jnp.maximum(drawn, -bound), bound).astype(kind)


def setup_inputs(seed: int = 0) -> dict:
    seeds = jax.random.split(jax.random.key(seed), 8)
    embeddings = normal_values(seeds[0], (USERS, D), 1.0, 6.0, ((0, 32),))
    cotangent = normal_values(seeds[1], (USERS, D), 1.0, 6.0, ((0, 32),))
    weight = normal_values(seeds[2], (D, D), D ** -0.5, 0.375)
    tiles = normal_values(seeds[3], (DEVICES_ALL, TILES_MAX, BLOCK, BLOCK), (max(BLOCK * TILES_MAX // 3, 1)) ** -0.5, 0.078125, ((0, 32),))
    tile_dst = with_ends(jax.random.randint(seeds[4], (DEVICES_ALL, TILES_MAX), 0, N_COL), jax.random.fold_in(seeds[4], 1), 0, N_COL - 1).astype(jnp.int32)
    tile_src = with_ends(jax.random.randint(seeds[5], (DEVICES_ALL, TILES_MAX), 0, N_ROW), jax.random.fold_in(seeds[5], 1), 0, N_ROW - 1).astype(jnp.int32)
    tile_count = draw_tile_count(jax.random.fold_in(seeds[7], 71), 0)
    return {"embeddings": embeddings, "cotangent": cotangent, "weight": weight, "tiles": tiles, "tile_dst": tile_dst, "tile_src": tile_src, "tile_count": tile_count}


def to_bfloat(values):
    return lax.optimization_barrier(values.astype(jnp.bfloat16)).astype(jnp.float32)

def reference(embeddings, cotangent, weight, tiles, tile_dst, tile_src, tile_count):
    highest = lax.Precision.HIGHEST
    slot_ids = jnp.arange(TILES_MAX, dtype=jnp.int32)
    column_ids = jnp.arange(N_COL, dtype=jnp.int32)
    row_ids = jnp.arange(N_ROW, dtype=jnp.int32)
    device_ids = jnp.arange(N_ROW * N_COL, dtype=jnp.int32)
    embed_grid = embeddings.reshape(N_ROW, N_COL, BLOCK, D)

    def forward_step(totals, inputs):
        device, block_tiles, dest_ids, source_ids, count = inputs
        row_index = device // N_COL
        column_index = device % N_COL
        source_group = lax.dynamic_index_in_dim(embed_grid, column_index, 1, keepdims=False)
        chosen = jnp.take(source_group, source_ids, axis=0).astype(jnp.float32)
        products = jnp.einsum('tij,tjd->tid', block_tiles.astype(jnp.float32), chosen, precision=highest)
        alive = (slot_ids < count).astype(jnp.float32)
        onehot = (dest_ids[:, None] == column_ids[None, :]).astype(jnp.float32) * alive[:, None]
        partial_value = to_bfloat(jnp.einsum('tc,tid->cid', onehot, products, precision=highest))
        current = lax.dynamic_index_in_dim(totals, row_index, 0, keepdims=False)
        totals = lax.dynamic_update_index_in_dim(totals, current + partial_value, row_index, 0)
        return (totals, None)
    start = jnp.zeros((N_ROW, N_COL, BLOCK, D), jnp.float32)
    totals, unused = lax.scan(forward_step, start, (device_ids, tiles, tile_dst, tile_src, tile_count))
    summed = totals.reshape(USERS, D)
    hidden = summed.astype(jnp.bfloat16)
    output = jnp.dot(hidden, weight, preferred_element_type=jnp.float32).astype(jnp.bfloat16)
    contract_rows = (((0,), (0,)), ((), ()))
    contract_cols = (((1,), (1,)), ((), ()))
    grad_weight = lax.dot_general(summed, cotangent.astype(jnp.float32), contract_rows, precision=highest) * (1.0 / math.sqrt(USERS))
    grad_hidden = lax.dot_general(cotangent, weight, contract_cols, preferred_element_type=jnp.float32).astype(jnp.bfloat16)
    grad_grid = grad_hidden.reshape(N_ROW, N_COL, BLOCK, D)

    def backward_step(totals, inputs):
        device, block_tiles, dest_ids, source_ids, count = inputs
        row_index = device // N_COL
        column_index = device % N_COL
        dest_group = lax.dynamic_index_in_dim(grad_grid, row_index, 0, keepdims=False)
        picked = jnp.take(dest_group, dest_ids, axis=0).astype(jnp.float32)
        products = jnp.einsum('tji,tjd->tid', block_tiles.astype(jnp.float32), picked, precision=highest)
        alive = (slot_ids < count).astype(jnp.float32)
        onehot = (source_ids[:, None] == row_ids[None, :]).astype(jnp.float32) * alive[:, None]
        partial_value = to_bfloat(jnp.einsum('tr,tid->rid', onehot, products, precision=highest))
        current = lax.dynamic_index_in_dim(totals, column_index, 1, keepdims=False)
        totals = lax.dynamic_update_index_in_dim(totals, current + partial_value, column_index, 1)
        return (totals, None)
    back_totals, unused_back = lax.scan(backward_step, start, (device_ids, tiles, tile_dst, tile_src, tile_count))
    grad_embeddings = back_totals.reshape(USERS, D).astype(jnp.bfloat16)
    return (output, grad_embeddings, grad_weight)
```

```python
import functools
import math

import jax
import jax.numpy as jnp
from jax import lax
from jax.experimental import pallas as pl
from jax.experimental.pallas import tpu as pltpu
from jax.sharding import PartitionSpec as P

F32 = jnp.float32
BF16 = jnp.bfloat16
ROWS_ROWS = (((0,), (0,)), ((), ()))
COLS_COLS = (((1,), (1,)), ((), ()))
CHUNKS = 4


def fused(
    n_row,
    n_col,
    link_ref,
    emb_ref,
    cot_ref,
    weight_ref,
    tiles_ref,
    out_ref,
    gemb_ref,
    gw_ref,
    tbuf,
    chain,
    a_rows,
    a_cols,
    e_all,
    c_all,
    part,
    part_in,
    back_sib,
    back_sib_in,
    back_own,
    back_sum,
    back_in,
    term,
    term_in,
    mid_in,
    fin,
    tile_sem,
    e_send,
    e_recv,
    relay_send,
    c_send,
    c_recv,
    p_send,
    p_recv,
    s_send,
    s_recv,
    b_send,
    b_recv,
    t_send,
    t_recv,
    m_send,
    m_recv,
    f_send,
    f_recv,
):
    block, width = emb_ref.shape
    slots = tiles_ref.shape[0]
    n_chip = n_row // 2
    row = lax.axis_index("row")
    col = lax.axis_index("col")
    core = lax.rem(row, 2)
    chip = row // 2
    sibling = row + 1 - 2 * core
    row_peers = [lax.rem(row + i, n_row) for i in range(1, n_row)]
    col_peers = [lax.rem(col + i, n_col) for i in range(1, n_col)]
    chip_peers = [lax.rem(chip + i, n_chip) for i in range(1, n_chip)]

    def remote(src, dst, send, recv, r, c):
        return pltpu.make_async_remote_copy(
            src_ref=src,
            dst_ref=dst,
            send_sem=send,
            recv_sem=recv,
            device_id=(r, c),
            device_id_type=pl.DeviceIdType.MESH,
        )

    sent = []

    def send(*args):
        copy = remote(*args)
        copy.start()
        sent.append(copy)

    def arrived(dst, sems, index):
        remote(dst.at[index], dst.at[index], sems.at[index], sems.at[index], sibling, col).wait_recv()

    per = slots // CHUNKS
    loads = []
    for i in range(CHUNKS):
        span = pl.ds(i * per, per)
        load = pltpu.make_async_copy(tiles_ref.at[span], tbuf.at[span], tile_sem.at[i])
        load.start()
        loads.append(load)

    barrier = pltpu.get_barrier_semaphore()
    for r in row_peers:
        pl.semaphore_signal(barrier, inc=1, device_id=(r, col), device_id_type=pl.DeviceIdType.MESH)
    for c in col_peers:
        pl.semaphore_signal(barrier, inc=1, device_id=(row, c), device_id_type=pl.DeviceIdType.MESH)
    pl.semaphore_wait(barrier, n_row + n_col - 2)

    for p in chip_peers:
        r = 2 * p + core
        send(emb_ref, e_all.at[row], e_send.at[r], e_recv.at[row], r, col)
    for c in col_peers:
        send(cot_ref, c_all.at[col], c_send.at[c], c_recv.at[col], row, c)
    send(emb_ref, e_all.at[row], e_send.at[sibling], e_recv.at[row], sibling, col)

    e_all[row] = emb_ref[...]
    c_all[col] = cot_ref[...]

    def relay(p):
        r = 2 * p + core
        arrived(e_all, e_recv, r)
        send(e_all.at[r], e_all.at[r], relay_send.at[r], e_recv.at[r], sibling, col)

    chain[0] = jnp.zeros((block, block), F32)

    def add_tile(t, carry):
        chain[t + 1] = tbuf[t].astype(F32) + chain[link_ref[t]]
        return carry

    waiting = list(chip_peers)
    for i in range(CHUNKS):
        loads[i].wait()
        lax.fori_loop(i * per, (i + 1) * per, add_tile, 0)
        if i > 0 and waiting:
            relay(waiting.pop(0))
    for p in waiting:
        relay(p)

    for k in range(n_col):
        for j in range(n_row):
            tile = chain[link_ref[slots + k * n_row + j]].astype(BF16)
            a_rows[k, :, pl.ds(j * block, block)] = tile
            a_cols[j, pl.ds(k * block, block), :] = tile

    arrived(e_all, e_recv, sibling)
    for p in chip_peers:
        arrived(e_all, e_recv, 2 * p + 1 - core)

    sources = e_all[...].reshape(n_row * block, width)
    for k in col_peers + [col]:
        part[k] = jnp.dot(a_rows[k], sources, preferred_element_type=F32).astype(BF16)
        if k is not col:
            send(part.at[k], part_in.at[col], p_send.at[k], p_recv.at[col], row, k)

    for c in col_peers:
        arrived(c_all, c_recv, c)
    cot_group = c_all[...].reshape(n_col * block, width)
    own_term = lax.dot_general(
        part[...].reshape(n_col * block, width), cot_group, ROWS_ROWS, preferred_element_type=F32
    )
    term[...] = own_term.astype(BF16).reshape(term.shape)
    for r in row_peers:
        send(term.at[r], term_in.at[row], t_send.at[r], t_recv.at[row], r, col)

    grad_hidden = lax.dot_general(
        cot_group, weight_ref[...], COLS_COLS, preferred_element_type=F32
    ).astype(BF16)

    def back(j):
        return lax.dot_general(a_cols[j], grad_hidden, ROWS_ROWS, preferred_element_type=F32)

    for p in chip_peers + [chip]:
        back_sib[p] = back(2 * p + 1 - core).astype(BF16)
        send(back_sib.at[p], back_sib_in.at[p], s_send.at[p], s_recv.at[p], sibling, col)
    for p in chip_peers + [chip]:
        back_own[p] = back(2 * p + core)

    for p in chip_peers:
        arrived(back_sib_in, s_recv, p)
        back_sum[p] = (back_own[p] + back_sib_in[p].astype(F32)).astype(BF16)
        send(back_sum.at[p], back_in.at[chip], b_send.at[p], b_recv.at[chip], 2 * p + core, col)

    row_sum = term[row].astype(F32)
    for r in row_peers:
        arrived(term_in, t_recv, r)
        row_sum = row_sum + term_in[r].astype(F32)
    mid_in[col] = row_sum.astype(BF16)
    for c in col_peers:
        send(mid_in.at[col], mid_in.at[col], m_send.at[c], m_recv.at[col], row, c)

    total = part[col].astype(F32)
    for c in col_peers:
        arrived(part_in, p_recv, c)
        total = total + part_in[c].astype(F32)
    out_ref[...] = jnp.dot(
        total.astype(BF16), weight_ref[...], preferred_element_type=F32
    ).astype(BF16)

    for c in col_peers:
        arrived(mid_in, m_recv, c)
    whole = mid_in[0].astype(F32)
    for c in range(1, n_col):
        whole = whole + mid_in[c].astype(F32)
    fin[row] = whole.astype(BF16)
    for r in row_peers:
        send(fin.at[row], fin.at[row], f_send.at[r], f_recv.at[row], r, col)

    arrived(back_sib_in, s_recv, chip)
    grad = back_own[chip] + back_sib_in[chip].astype(F32)
    for p in chip_peers:
        arrived(back_in, b_recv, p)
        grad = grad + back_in[p].astype(F32)
    gemb_ref[...] = grad.astype(BF16)

    for r in row_peers:
        arrived(fin, f_recv, r)
    scale = 1.0 / math.sqrt(block * n_row * n_col)
    gw_ref[...] = fin[...].reshape(gw_ref.shape).astype(F32) * scale

    for copy in sent:
        copy.wait_send()


def combined(n_row, n_col, embeddings, cotangent, weight, tiles, tile_dst, tile_src, tile_count):
    block, width = embeddings.shape
    slots = tiles.shape[1]
    pairs = n_row * n_col
    n_chip = n_row // 2
    strip = weight.shape[0] // n_row
    place = jnp.arange(slots, dtype=jnp.int32)
    code = jnp.where(place < tile_count[0], tile_dst[0] * n_row + tile_src[0], -1)
    asked = jnp.concatenate([code, jnp.arange(pairs, dtype=jnp.int32)])
    limit = jnp.minimum(jnp.arange(slots + pairs, dtype=jnp.int32), slots)
    same = (code[None, :] == asked[:, None]) & (place[None, :] < limit[:, None])
    link = jnp.max(jnp.where(same, place[None, :] + 1, 0), axis=1)

    vmem = pl.BlockSpec(memory_space=pltpu.VMEM)
    dma = pltpu.SemaphoreType.DMA
    return pl.pallas_call(
        functools.partial(fused, n_row, n_col),
        out_shape=(
            jax.ShapeDtypeStruct((block, width), BF16),
            jax.ShapeDtypeStruct((block, width), BF16),
            jax.ShapeDtypeStruct(weight.shape, F32),
        ),
        in_specs=[
            pl.BlockSpec(memory_space=pltpu.SMEM),
            vmem,
            vmem,
            vmem,
            pl.BlockSpec(memory_space=pl.ANY),
        ],
        out_specs=(vmem, vmem, vmem),
        scratch_shapes=[
            pltpu.VMEM((slots, block, block), BF16),
            pltpu.VMEM((slots + 1, block, block), F32),
            pltpu.VMEM((n_col, block, n_row * block), BF16),
            pltpu.VMEM((n_row, n_col * block, block), BF16),
            pltpu.VMEM((n_row, block, width), BF16),
            pltpu.VMEM((n_col, block, width), BF16),
            pltpu.VMEM((n_col, block, width), BF16),
            pltpu.VMEM((n_col, block, width), BF16),
            pltpu.VMEM((n_chip, block, width), BF16),
            pltpu.VMEM((n_chip, block, width), BF16),
            pltpu.VMEM((n_chip, block, width), F32),
            pltpu.VMEM((n_chip, block, width), BF16),
            pltpu.VMEM((n_chip, block, width), BF16),
            pltpu.VMEM((n_row, strip, width), BF16),
            pltpu.VMEM((n_row, strip, width), BF16),
            pltpu.VMEM((n_col, strip, width), BF16),
            pltpu.VMEM((n_row, strip, width), BF16),
            dma((CHUNKS,)),
            dma((n_row,)),
            dma((n_row,)),
            dma((n_row,)),
            dma((n_col,)),
            dma((n_col,)),
            dma((n_col,)),
            dma((n_col,)),
            dma((n_chip,)),
            dma((n_chip,)),
            dma((n_chip,)),
            dma((n_chip,)),
            dma((n_row,)),
            dma((n_row,)),
            dma((n_col,)),
            dma((n_col,)),
            dma((n_row,)),
            dma((n_row,)),
        ],
        compiler_params=pltpu.CompilerParams(
            collective_id=0, has_side_effects=True, vmem_limit_bytes=40 * 1024 * 1024
        ),
    )(link, embeddings, cotangent, weight, tiles[0])


def slotwise(n_row, n_col, embeddings, cotangent, weight, tiles, tile_dst, tile_src, tile_count):
    block, width = embeddings.shape
    gathered = lax.all_gather(embeddings, "row", axis=0)
    grad_hidden = lax.dot_general(
        cotangent, weight, COLS_COLS, preferred_element_type=F32
    ).astype(BF16)
    grad_group = lax.all_gather(grad_hidden, "col", axis=0)

    def add_slot(t, sums):
        forward, backward = sums
        k, j = tile_dst[0, t], tile_src[0, t]
        tile = lax.dynamic_index_in_dim(tiles[0], t, 0, keepdims=False)
        source = lax.dynamic_index_in_dim(gathered, j, 0, keepdims=False)
        grad = lax.dynamic_index_in_dim(grad_group, k, 0, keepdims=False)
        ahead = jnp.dot(tile, source, preferred_element_type=F32)
        behind = lax.dot_general(tile, grad, ROWS_ROWS, preferred_element_type=F32)
        ahead = ahead + lax.dynamic_index_in_dim(forward, k, 0, keepdims=False)
        behind = behind + lax.dynamic_index_in_dim(backward, j, 0, keepdims=False)
        return (
            lax.dynamic_update_index_in_dim(forward, ahead, k, 0),
            lax.dynamic_update_index_in_dim(backward, behind, j, 0),
        )

    zeros = (jnp.zeros((n_col, block, width), F32), jnp.zeros((n_row, block, width), F32))
    forward, backward = lax.fori_loop(0, tile_count[0], add_slot, zeros)
    summed = lax.psum_scatter(
        forward.astype(BF16).reshape(n_col * block, width), "col", scatter_dimension=0, tiled=True
    ).astype(F32)
    output = jnp.dot(summed.astype(BF16), weight, preferred_element_type=F32).astype(BF16)
    term = lax.dot_general(
        summed, cotangent.astype(F32), ROWS_ROWS, precision=lax.Precision.HIGHEST
    )
    grad_weight = lax.psum(term, ("row", "col")) * (1.0 / math.sqrt(block * n_row * n_col))
    grad_embeddings = lax.psum_scatter(
        backward.astype(BF16).reshape(n_row * block, width), "row", scatter_dimension=0, tiled=True
    )
    return (output, grad_embeddings, grad_weight)


def solution(mesh):
    n_row, n_col = mesh.shape["row"], mesh.shape["col"]

    def local(embeddings, cotangent, weight, tiles, tile_dst, tile_src, tile_count):
        fits = n_row * n_col <= tiles.shape[1] and n_row % 2 == 0
        fits = fits and tiles.shape[1] % CHUNKS == 0 and weight.shape[0] % (16 * n_row) == 0
        body = functools.partial(combined if fits else slotwise, n_row, n_col)
        return body(embeddings, cotangent, weight, tiles, tile_dst, tile_src, tile_count)

    in_specs = (
        P(("row", "col"), None),
        P(("row", "col"), None),
        P(),
        P(("row", "col"), None, None, None),
        P(("row", "col"), None),
        P(("row", "col"), None),
        P(("row", "col")),
    )
    out_specs = (P(("row", "col"), None), P(("row", "col"), None), P())
    return jax.shard_map(local, mesh=mesh, in_specs=in_specs, out_specs=out_specs, check_vma=False)
```

```python
import functools
import math

import jax
import jax.numpy as jnp
from jax import lax
from jax.experimental import pallas as pl
from jax.experimental.pallas import tpu as pltpu
from jax.sharding import PartitionSpec as P

F32 = jnp.float32
BF16 = jnp.bfloat16
ROWS_ROWS = (((0,), (0,)), ((), ()))
COLS_COLS = (((1,), (1,)), ((), ()))
CHUNKS = 4


def fused(
    n_row,
    n_col,
    count_ref,
    dst_ref,
    src_ref,
    emb_ref,
    cot_ref,
    weight_ref,
    tiles_ref,
    out_ref,
    gemb_ref,
    gw_ref,
    link_v,
    link_ref,
    wbuf,
    tbuf,
    chain,
    a_rows,
    a_cols,
    e_all,
    c_all,
    part,
    part_in,
    back_sib,
    back_sib_in,
    back_own,
    back_sum,
    back_in,
    term,
    term_in,
    mid_in,
    fin,
    link_sem,
    own_sem,
    tile_sem,
    e_send,
    e_recv,
    relay_send,
    c_send,
    c_recv,
    p_send,
    p_recv,
    s_send,
    s_recv,
    b_send,
    b_recv,
    t_send,
    t_recv,
    m_send,
    m_recv,
    f_send,
    f_recv,
):
    block, width = emb_ref.shape
    slots = tiles_ref.shape[0]
    n_chip = n_row // 2
    row = lax.axis_index("row")
    col = lax.axis_index("col")
    core = lax.rem(row, 2)
    chip = row // 2
    sibling = row + 1 - 2 * core
    row_peers = [lax.rem(row + i, n_row) for i in range(1, n_row)]
    col_peers = [lax.rem(col + i, n_col) for i in range(1, n_col)]
    chip_peers = [lax.rem(chip + i, n_chip) for i in range(1, n_chip)]

    def remote(src, dst, send, recv, r, c):
        return pltpu.make_async_remote_copy(
            src_ref=src,
            dst_ref=dst,
            send_sem=send,
            recv_sem=recv,
            device_id=(r, c),
            device_id_type=pl.DeviceIdType.MESH,
        )

    sent = []

    def send(*args):
        copy = remote(*args)
        copy.start()
        sent.append(copy)

    def arrived(dst, sems, index):
        remote(dst.at[index], dst.at[index], sems.at[index], sems.at[index], sibling, col).wait_recv()

    owned = [(emb_ref, e_all.at[row]), (cot_ref, c_all.at[col]), (weight_ref, wbuf)]
    owned = [pltpu.make_async_copy(a, b, own_sem.at[i]) for i, (a, b) in enumerate(owned)]
    for copy in owned:
        copy.start()
    per = slots // CHUNKS
    loads = []
    for i in range(CHUNKS):
        span = pl.ds(i * per, per)
        load = pltpu.make_async_copy(tiles_ref.at[span], tbuf.at[span], tile_sem.at[i])
        load.start()
        loads.append(load)

    barrier = pltpu.get_barrier_semaphore()
    for r in row_peers:
        pl.semaphore_signal(barrier, inc=1, device_id=(r, col), device_id_type=pl.DeviceIdType.MESH)
    for c in col_peers:
        pl.semaphore_signal(barrier, inc=1, device_id=(row, c), device_id_type=pl.DeviceIdType.MESH)
    pl.semaphore_wait(barrier, n_row + n_col - 2)

    for p in chip_peers:
        r = 2 * p + core
        send(emb_ref, e_all.at[row], e_send.at[r], e_recv.at[row], r, col)
    for c in col_peers:
        send(cot_ref, c_all.at[col], c_send.at[c], c_recv.at[col], row, c)
    send(emb_ref, e_all.at[row], e_send.at[sibling], e_recv.at[row], sibling, col)

    for copy in owned:
        copy.wait()

    def relay(p):
        r = 2 * p + core
        arrived(e_all, e_recv, r)
        send(e_all.at[r], e_all.at[r], relay_send.at[r], e_recv.at[r], sibling, col)

    spot = lax.broadcasted_iota(jnp.int32, (1, slots), 1)
    code = jnp.where(spot < count_ref[0], dst_ref[...] * n_row + src_ref[...], -1)
    down = jnp.broadcast_to(code, (slots, slots)).T
    ahead = lax.broadcasted_iota(jnp.int32, (slots, slots), 0)
    before = (down == code) & (ahead < lax.broadcasted_iota(jnp.int32, (slots, slots), 1))
    link_v[0:1, :] = jnp.max(jnp.where(before, ahead + 1, 0), axis=0, keepdims=True)
    ends = down == lax.broadcasted_iota(jnp.int32, (slots, slots), 1)
    link_v[1:2, :] = jnp.max(jnp.where(ends, ahead + 1, 0), axis=0, keepdims=True)
    links = pltpu.make_async_copy(link_v, link_ref, link_sem)
    links.start()
    links.wait()

    chain[0] = jnp.zeros((block, block), F32)

    def add_tile(t, carry):
        chain[t + 1] = tbuf[t].astype(F32) + chain[link_ref[0, t]]
        return carry

    waiting = list(chip_peers)
    for i in range(CHUNKS):
        loads[i].wait()
        lax.fori_loop(i * per, (i + 1) * per, add_tile, 0, unroll=4)
        if i > 0 and waiting:
            relay(waiting.pop(0))
    for p in waiting:
        relay(p)

    for k in range(n_col):
        for j in range(n_row):
            tile = chain[link_ref[1, k * n_row + j]].astype(BF16)
            a_rows[k, :, pl.ds(j * block, block)] = tile
            a_cols[j, pl.ds(k * block, block), :] = tile

    arrived(e_all, e_recv, sibling)
    for p in chip_peers:
        arrived(e_all, e_recv, 2 * p + 1 - core)

    sources = e_all[...].reshape(n_row * block, width)
    for k in col_peers + [col]:
        part[k] = jnp.dot(a_rows[k], sources, preferred_element_type=F32).astype(BF16)

    for c in col_peers:
        arrived(c_all, c_recv, c)
    cot_group = c_all[...].reshape(n_col * block, width)
    own_term = lax.dot_general(
        part[...].reshape(n_col * block, width), cot_group, ROWS_ROWS, preferred_element_type=F32
    )
    term[...] = own_term.astype(BF16).reshape(term.shape)
    for r in row_peers:
        send(term.at[r], term_in.at[row], t_send.at[r], t_recv.at[row], r, col)

    grad_hidden = lax.dot_general(
        cot_group, wbuf[...], COLS_COLS, preferred_element_type=F32
    ).astype(BF16)

    def back(j):
        return lax.dot_general(a_cols[j], grad_hidden, ROWS_ROWS, preferred_element_type=F32)

    for p in chip_peers + [chip]:
        back_sib[p] = back(2 * p + 1 - core).astype(BF16)
        send(back_sib.at[p], back_sib_in.at[p], s_send.at[p], s_recv.at[p], sibling, col)
    row_sum = term[row].astype(F32)
    for r in row_peers:
        arrived(term_in, t_recv, r)
        row_sum = row_sum + term_in[r].astype(F32)
    mid_in[col] = row_sum.astype(BF16)
    for c in col_peers:
        send(mid_in.at[col], mid_in.at[col], m_send.at[c], m_recv.at[col], row, c)

    for k in col_peers:
        send(part.at[k], part_in.at[col], p_send.at[k], p_recv.at[col], row, k)

    for p in chip_peers + [chip]:
        back_own[p] = back(2 * p + core)

    for p in chip_peers:
        arrived(back_sib_in, s_recv, p)
        back_sum[p] = (back_own[p] + back_sib_in[p].astype(F32)).astype(BF16)
        send(back_sum.at[p], back_in.at[chip], b_send.at[p], b_recv.at[chip], 2 * p + core, col)

    for c in col_peers:
        arrived(mid_in, m_recv, c)
    whole = mid_in[0].astype(F32)
    for c in range(1, n_col):
        whole = whole + mid_in[c].astype(F32)
    fin[row] = whole.astype(BF16)
    for r in row_peers:
        send(fin.at[row], fin.at[row], f_send.at[r], f_recv.at[row], r, col)

    total = part[col].astype(F32)
    for c in col_peers:
        arrived(part_in, p_recv, c)
        total = total + part_in[c].astype(F32)
    out_ref[...] = jnp.dot(
        total.astype(BF16), wbuf[...], preferred_element_type=F32
    ).astype(BF16)

    arrived(back_sib_in, s_recv, chip)
    grad = back_own[chip] + back_sib_in[chip].astype(F32)
    for p in chip_peers:
        arrived(back_in, b_recv, p)
        grad = grad + back_in[p].astype(F32)
    gemb_ref[...] = grad.astype(BF16)

    for r in row_peers:
        arrived(fin, f_recv, r)
    scale = 1.0 / math.sqrt(block * n_row * n_col)
    gw_ref[...] = fin[...].reshape(gw_ref.shape).astype(F32) * scale

    for copy in sent:
        copy.wait_send()


def hand_over(*refs):
    read, write = refs[-2:]
    reads = [pltpu.make_async_copy(refs[i], refs[i + 6], read.at[i]) for i in range(3)]
    writes = [pltpu.make_async_copy(refs[i + 6], refs[i + 3], write.at[i]) for i in range(3)]
    for copy in reads:
        copy.start()
    for i in range(3):
        reads[i].wait()
        writes[i].start()
    for copy in writes:
        copy.wait()


def combined(n_row, n_col, embeddings, cotangent, weight, tiles, tile_dst, tile_src, tile_count):
    block, width = embeddings.shape
    slots = tiles.shape[1]
    pairs = n_row * n_col
    n_chip = n_row // 2
    strip = weight.shape[0] // n_row
    vmem = pl.BlockSpec(memory_space=pltpu.VMEM)
    whole = pl.BlockSpec(memory_space=pl.ANY)
    dma = pltpu.SemaphoreType.DMA
    results = pl.pallas_call(
        functools.partial(fused, n_row, n_col),
        out_shape=(
            jax.ShapeDtypeStruct((block, width), BF16),
            jax.ShapeDtypeStruct((block, width), BF16),
            jax.ShapeDtypeStruct(weight.shape, F32),
        ),
        in_specs=[
            pl.BlockSpec(memory_space=pltpu.SMEM),
            vmem,
            vmem,
            whole,
            whole,
            whole,
            whole,
        ],
        out_specs=(vmem, vmem, vmem),
        scratch_shapes=[
            pltpu.VMEM((2, slots), jnp.int32),
            pltpu.SMEM((2, slots), jnp.int32),
            pltpu.VMEM(weight.shape, BF16),
            pltpu.VMEM((slots, block, block), BF16),
            pltpu.VMEM((slots + 1, block, block), F32),
            pltpu.VMEM((n_col, block, n_row * block), BF16),
            pltpu.VMEM((n_row, n_col * block, block), BF16),
            pltpu.VMEM((n_row, block, width), BF16),
            pltpu.VMEM((n_col, block, width), BF16),
            pltpu.VMEM((n_col, block, width), BF16),
            pltpu.VMEM((n_col, block, width), BF16),
            pltpu.VMEM((n_chip, block, width), BF16),
            pltpu.VMEM((n_chip, block, width), BF16),
            pltpu.VMEM((n_chip, block, width), F32),
            pltpu.VMEM((n_chip, block, width), BF16),
            pltpu.VMEM((n_chip, block, width), BF16),
            pltpu.VMEM((n_row, strip, width), BF16),
            pltpu.VMEM((n_row, strip, width), BF16),
            pltpu.VMEM((n_col, strip, width), BF16),
            pltpu.VMEM((n_row, strip, width), BF16),
            dma,
            dma((3,)),
            dma((CHUNKS,)),
            dma((n_row,)),
            dma((n_row,)),
            dma((n_row,)),
            dma((n_col,)),
            dma((n_col,)),
            dma((n_col,)),
            dma((n_col,)),
            dma((n_chip,)),
            dma((n_chip,)),
            dma((n_chip,)),
            dma((n_chip,)),
            dma((n_row,)),
            dma((n_row,)),
            dma((n_col,)),
            dma((n_col,)),
            dma((n_row,)),
            dma((n_row,)),
        ],
        compiler_params=pltpu.CompilerParams(
            collective_id=0, has_side_effects=True, vmem_limit_bytes=60 * 1024 * 1024
        ),
    )(tile_count, tile_dst, tile_src, embeddings, cotangent, weight, tiles[0])
    return pl.pallas_call(
        hand_over,
        out_shape=tuple(jax.ShapeDtypeStruct(x.shape, x.dtype) for x in results),
        in_specs=[whole] * 3,
        out_specs=(whole,) * 3,
        scratch_shapes=[pltpu.VMEM(x.shape, x.dtype) for x in results] + [dma((3,)), dma((3,))],
    )(*results)


def slotwise(n_row, n_col, embeddings, cotangent, weight, tiles, tile_dst, tile_src, tile_count):
    block, width = embeddings.shape
    gathered = lax.all_gather(embeddings, "row", axis=0)
    grad_hidden = lax.dot_general(
        cotangent, weight, COLS_COLS, preferred_element_type=F32
    ).astype(BF16)
    grad_group = lax.all_gather(grad_hidden, "col", axis=0)

    def add_slot(t, sums):
        forward, backward = sums
        k, j = tile_dst[0, t], tile_src[0, t]
        tile = lax.dynamic_index_in_dim(tiles[0], t, 0, keepdims=False)
        source = lax.dynamic_index_in_dim(gathered, j, 0, keepdims=False)
        grad = lax.dynamic_index_in_dim(grad_group, k, 0, keepdims=False)
        ahead = jnp.dot(tile, source, preferred_element_type=F32)
        behind = lax.dot_general(tile, grad, ROWS_ROWS, preferred_element_type=F32)
        ahead = ahead + lax.dynamic_index_in_dim(forward, k, 0, keepdims=False)
        behind = behind + lax.dynamic_index_in_dim(backward, j, 0, keepdims=False)
        return (
            lax.dynamic_update_index_in_dim(forward, ahead, k, 0),
            lax.dynamic_update_index_in_dim(backward, behind, j, 0),
        )

    zeros = (jnp.zeros((n_col, block, width), F32), jnp.zeros((n_row, block, width), F32))
    forward, backward = lax.fori_loop(0, tile_count[0], add_slot, zeros)
    summed = lax.psum_scatter(
        forward.astype(BF16).reshape(n_col * block, width), "col", scatter_dimension=0, tiled=True
    ).astype(F32)
    output = jnp.dot(summed.astype(BF16), weight, preferred_element_type=F32).astype(BF16)
    term = lax.dot_general(
        summed, cotangent.astype(F32), ROWS_ROWS, precision=lax.Precision.HIGHEST
    )
    grad_weight = lax.psum(term, ("row", "col")) * (1.0 / math.sqrt(block * n_row * n_col))
    grad_embeddings = lax.psum_scatter(
        backward.astype(BF16).reshape(n_row * block, width), "row", scatter_dimension=0, tiled=True
    )
    return (output, grad_embeddings, grad_weight)


def solution(mesh):
    n_row, n_col = mesh.shape["row"], mesh.shape["col"]

    def local(embeddings, cotangent, weight, tiles, tile_dst, tile_src, tile_count):
        fits = n_row * n_col <= tiles.shape[1] and n_row % 2 == 0
        fits = fits and tiles.shape[1] % CHUNKS == 0 and weight.shape[0] % (16 * n_row) == 0
        body = functools.partial(combined if fits else slotwise, n_row, n_col)
        return body(embeddings, cotangent, weight, tiles, tile_dst, tile_src, tile_count)

    in_specs = (
        P(("row", "col"), None),
        P(("row", "col"), None),
        P(),
        P(("row", "col"), None, None, None),
        P(("row", "col"), None),
        P(("row", "col"), None),
        P(("row", "col")),
    )
    out_specs = (P(("row", "col"), None), P(("row", "col"), None), P())
    return jax.shard_map(local, mesh=mesh, in_specs=in_specs, out_specs=out_specs, check_vma=False)
```

```python
import functools
import math

import jax
import jax.numpy as jnp
from jax import lax
from jax.experimental import pallas as pl
from jax.experimental.pallas import tpu as pltpu
from jax.sharding import PartitionSpec as P

F32 = jnp.float32
BF16 = jnp.bfloat16
ROWS_ROWS = (((0,), (0,)), ((), ()))
COLS_COLS = (((1,), (1,)), ((), ()))
CHUNKS = 4


def fused(
    n_row,
    n_col,
    count_ref,
    dst_ref,
    src_ref,
    emb_ref,
    cot_ref,
    weight_ref,
    tiles_ref,
    out_ref,
    gemb_ref,
    gw_ref,
    link_v,
    link_ref,
    wbuf,
    tbuf,
    chain,
    a_rows,
    a_cols,
    e_all,
    c_all,
    part,
    part_in,
    back_sib,
    back_sib_in,
    back_own,
    back_sum,
    back_in,
    term,
    term_in,
    mid_in,
    fin,
    link_sem,
    own_sem,
    tile_sem,
    e_send,
    e_recv,
    relay_send,
    c_send,
    c_recv,
    p_send,
    p_recv,
    s_send,
    s_recv,
    b_send,
    b_recv,
    t_send,
    t_recv,
    m_send,
    m_recv,
    f_send,
    f_recv,
):
    block, width = emb_ref.shape
    slots = tiles_ref.shape[0]
    n_chip = n_row // 2
    row = lax.axis_index("row")
    col = lax.axis_index("col")
    core = lax.rem(row, 2)
    chip = row // 2
    sibling = row + 1 - 2 * core
    row_peers = [lax.rem(row + i, n_row) for i in range(1, n_row)]
    col_peers = [lax.rem(col + i, n_col) for i in range(1, n_col)]
    chip_peers = [lax.rem(chip + i, n_chip) for i in range(1, n_chip)]

    def remote(src, dst, send, recv, r, c):
        return pltpu.make_async_remote_copy(
            src_ref=src,
            dst_ref=dst,
            send_sem=send,
            recv_sem=recv,
            device_id=(r, c),
            device_id_type=pl.DeviceIdType.MESH,
        )

    sent = []

    def send(*args):
        copy = remote(*args)
        copy.start()
        sent.append(copy)

    def arrived(dst, sems, index):
        remote(dst.at[index], dst.at[index], sems.at[index], sems.at[index], sibling, col).wait_recv()

    owned = [(emb_ref, e_all.at[row]), (cot_ref, c_all.at[col]), (weight_ref, wbuf)]
    owned = [pltpu.make_async_copy(a, b, own_sem.at[i]) for i, (a, b) in enumerate(owned)]
    for copy in owned:
        copy.start()
    per = slots // CHUNKS
    loads = []
    for i in range(CHUNKS):
        span = pl.ds(i * per, per)
        load = pltpu.make_async_copy(tiles_ref.at[span], tbuf.at[span], tile_sem.at[i])
        load.start()
        loads.append(load)

    barrier = pltpu.get_barrier_semaphore()
    for r in row_peers:
        pl.semaphore_signal(barrier, inc=1, device_id=(r, col), device_id_type=pl.DeviceIdType.MESH)
    for c in col_peers:
        pl.semaphore_signal(barrier, inc=1, device_id=(row, c), device_id_type=pl.DeviceIdType.MESH)
    pl.semaphore_wait(barrier, n_row + n_col - 2)

    for p in chip_peers:
        r = 2 * p + core
        send(emb_ref, e_all.at[row], e_send.at[r], e_recv.at[row], r, col)
    for c in col_peers:
        send(cot_ref, c_all.at[col], c_send.at[c], c_recv.at[col], row, c)
    send(emb_ref, e_all.at[row], e_send.at[sibling], e_recv.at[row], sibling, col)

    for copy in owned:
        copy.wait()

    def relay(p):
        r = 2 * p + core
        arrived(e_all, e_recv, r)
        send(e_all.at[r], e_all.at[r], relay_send.at[r], e_recv.at[r], sibling, col)

    spot = lax.broadcasted_iota(jnp.int32, (1, slots), 1)
    code = jnp.where(spot < count_ref[0], dst_ref[...] * n_row + src_ref[...], -1)
    down = jnp.broadcast_to(code, (slots, slots)).T
    ahead = lax.broadcasted_iota(jnp.int32, (slots, slots), 0)
    before = (down == code) & (ahead < lax.broadcasted_iota(jnp.int32, (slots, slots), 1))
    link_v[0:1, :] = jnp.max(jnp.where(before, ahead + 1, 0), axis=0, keepdims=True)
    ends = down == lax.broadcasted_iota(jnp.int32, (slots, slots), 1)
    link_v[1:2, :] = jnp.max(jnp.where(ends, ahead + 1, 0), axis=0, keepdims=True)
    links = pltpu.make_async_copy(link_v, link_ref, link_sem)
    links.start()
    links.wait()

    chain[0] = jnp.zeros((block, block), F32)

    def add_tile(t, carry):
        chain[t + 1] = tbuf[t].astype(F32) + chain[link_ref[0, t]]
        return carry

    for i in range(CHUNKS):
        loads[i].wait()
        lax.fori_loop(i * per, (i + 1) * per, add_tile, 0, unroll=4)
    for p in chip_peers:
        relay(p)

    for k in range(n_col):
        for j in range(n_row):
            tile = chain[link_ref[1, k * n_row + j]].astype(BF16)
            a_rows[k, :, pl.ds(j * block, block)] = tile
            a_cols[j, pl.ds(k * block, block), :] = tile

    arrived(e_all, e_recv, sibling)
    for p in chip_peers:
        arrived(e_all, e_recv, 2 * p + 1 - core)

    sources = e_all[...].reshape(n_row * block, width)
    for k in col_peers + [col]:
        part[k] = jnp.dot(a_rows[k], sources, preferred_element_type=F32).astype(BF16)

    for c in col_peers:
        arrived(c_all, c_recv, c)
    cot_group = c_all[...].reshape(n_col * block, width)
    own_term = lax.dot_general(
        part[...].reshape(n_col * block, width), cot_group, ROWS_ROWS, preferred_element_type=F32
    )
    term[...] = own_term.astype(BF16).reshape(term.shape)
    for r in row_peers:
        send(term.at[r], term_in.at[row], t_send.at[r], t_recv.at[row], r, col)

    for k in col_peers[:2]:
        send(part.at[k], part_in.at[col], p_send.at[k], p_recv.at[col], row, k)

    grad_hidden = lax.dot_general(
        cot_group, wbuf[...], COLS_COLS, preferred_element_type=F32
    ).astype(BF16)

    def back(j):
        return lax.dot_general(a_cols[j], grad_hidden, ROWS_ROWS, preferred_element_type=F32)

    for p in chip_peers + [chip]:
        back_sib[p] = back(2 * p + 1 - core).astype(BF16)
        send(back_sib.at[p], back_sib_in.at[p], s_send.at[p], s_recv.at[p], sibling, col)
    row_sum = term[row].astype(F32)
    for r in row_peers:
        arrived(term_in, t_recv, r)
        row_sum = row_sum + term_in[r].astype(F32)
    mid_in[col] = row_sum.astype(BF16)
    for c in col_peers:
        send(mid_in.at[col], mid_in.at[col], m_send.at[c], m_recv.at[col], row, c)

    for k in col_peers[2:]:
        send(part.at[k], part_in.at[col], p_send.at[k], p_recv.at[col], row, k)

    for p in chip_peers + [chip]:
        back_own[p] = back(2 * p + core)

    for p in chip_peers:
        arrived(back_sib_in, s_recv, p)
        back_sum[p] = (back_own[p] + back_sib_in[p].astype(F32)).astype(BF16)
        send(back_sum.at[p], back_in.at[chip], b_send.at[p], b_recv.at[chip], 2 * p + core, col)

    for c in col_peers:
        arrived(mid_in, m_recv, c)
    whole = mid_in[0].astype(F32)
    for c in range(1, n_col):
        whole = whole + mid_in[c].astype(F32)
    fin[row] = whole.astype(BF16)
    for r in row_peers:
        send(fin.at[row], fin.at[row], f_send.at[r], f_recv.at[row], r, col)

    total = part[col].astype(F32)
    for c in col_peers:
        arrived(part_in, p_recv, c)
        total = total + part_in[c].astype(F32)
    out_ref[...] = jnp.dot(
        total.astype(BF16), wbuf[...], preferred_element_type=F32
    ).astype(BF16)

    arrived(back_sib_in, s_recv, chip)
    grad = back_own[chip] + back_sib_in[chip].astype(F32)
    for p in chip_peers:
        arrived(back_in, b_recv, p)
        grad = grad + back_in[p].astype(F32)
    gemb_ref[...] = grad.astype(BF16)

    for r in row_peers:
        arrived(fin, f_recv, r)
    scale = 1.0 / math.sqrt(block * n_row * n_col)
    gw_ref[...] = fin[...].reshape(gw_ref.shape).astype(F32) * scale

    for copy in sent:
        copy.wait_send()


def hand_over(*refs):
    read, write = refs[-2:]
    reads = [pltpu.make_async_copy(refs[i], refs[i + 6], read.at[i]) for i in range(3)]
    writes = [pltpu.make_async_copy(refs[i + 6], refs[i + 3], write.at[i]) for i in range(3)]
    for copy in reads:
        copy.start()
    for i in range(3):
        reads[i].wait()
        writes[i].start()
    for copy in writes:
        copy.wait()


def combined(n_row, n_col, embeddings, cotangent, weight, tiles, tile_dst, tile_src, tile_count):
    block, width = embeddings.shape
    slots = tiles.shape[1]
    pairs = n_row * n_col
    n_chip = n_row // 2
    strip = weight.shape[0] // n_row
    vmem = pl.BlockSpec(memory_space=pltpu.VMEM)
    whole = pl.BlockSpec(memory_space=pl.ANY)
    dma = pltpu.SemaphoreType.DMA
    results = pl.pallas_call(
        functools.partial(fused, n_row, n_col),
        out_shape=(
            jax.ShapeDtypeStruct((block, width), BF16),
            jax.ShapeDtypeStruct((block, width), BF16),
            jax.ShapeDtypeStruct(weight.shape, F32),
        ),
        in_specs=[
            pl.BlockSpec(memory_space=pltpu.SMEM),
            vmem,
            vmem,
            whole,
            whole,
            whole,
            whole,
        ],
        out_specs=(vmem, vmem, vmem),
        scratch_shapes=[
            pltpu.VMEM((2, slots), jnp.int32),
            pltpu.SMEM((2, slots), jnp.int32),
            pltpu.VMEM(weight.shape, BF16),
            pltpu.VMEM((slots, block, block), BF16),
            pltpu.VMEM((slots + 1, block, block), F32),
            pltpu.VMEM((n_col, block, n_row * block), BF16),
            pltpu.VMEM((n_row, n_col * block, block), BF16),
            pltpu.VMEM((n_row, block, width), BF16),
            pltpu.VMEM((n_col, block, width), BF16),
            pltpu.VMEM((n_col, block, width), BF16),
            pltpu.VMEM((n_col, block, width), BF16),
            pltpu.VMEM((n_chip, block, width), BF16),
            pltpu.VMEM((n_chip, block, width), BF16),
            pltpu.VMEM((n_chip, block, width), F32),
            pltpu.VMEM((n_chip, block, width), BF16),
            pltpu.VMEM((n_chip, block, width), BF16),
            pltpu.VMEM((n_row, strip, width), BF16),
            pltpu.VMEM((n_row, strip, width), BF16),
            pltpu.VMEM((n_col, strip, width), BF16),
            pltpu.VMEM((n_row, strip, width), BF16),
            dma,
            dma((3,)),
            dma((CHUNKS,)),
            dma((n_row,)),
            dma((n_row,)),
            dma((n_row,)),
            dma((n_col,)),
            dma((n_col,)),
            dma((n_col,)),
            dma((n_col,)),
            dma((n_chip,)),
            dma((n_chip,)),
            dma((n_chip,)),
            dma((n_chip,)),
            dma((n_row,)),
            dma((n_row,)),
            dma((n_col,)),
            dma((n_col,)),
            dma((n_row,)),
            dma((n_row,)),
        ],
        compiler_params=pltpu.CompilerParams(
            collective_id=0, has_side_effects=True, vmem_limit_bytes=60 * 1024 * 1024
        ),
    )(tile_count, tile_dst, tile_src, embeddings, cotangent, weight, tiles[0])
    return pl.pallas_call(
        hand_over,
        out_shape=tuple(jax.ShapeDtypeStruct(x.shape, x.dtype) for x in results),
        in_specs=[whole] * 3,
        out_specs=(whole,) * 3,
        scratch_shapes=[pltpu.VMEM(x.shape, x.dtype) for x in results] + [dma((3,)), dma((3,))],
    )(*results)


def slotwise(n_row, n_col, embeddings, cotangent, weight, tiles, tile_dst, tile_src, tile_count):
    block, width = embeddings.shape
    gathered = lax.all_gather(embeddings, "row", axis=0)
    grad_hidden = lax.dot_general(
        cotangent, weight, COLS_COLS, preferred_element_type=F32
    ).astype(BF16)
    grad_group = lax.all_gather(grad_hidden, "col", axis=0)

    def add_slot(t, sums):
        forward, backward = sums
        k, j = tile_dst[0, t], tile_src[0, t]
        tile = lax.dynamic_index_in_dim(tiles[0], t, 0, keepdims=False)
        source = lax.dynamic_index_in_dim(gathered, j, 0, keepdims=False)
        grad = lax.dynamic_index_in_dim(grad_group, k, 0, keepdims=False)
        ahead = jnp.dot(tile, source, preferred_element_type=F32)
        behind = lax.dot_general(tile, grad, ROWS_ROWS, preferred_element_type=F32)
        ahead = ahead + lax.dynamic_index_in_dim(forward, k, 0, keepdims=False)
        behind = behind + lax.dynamic_index_in_dim(backward, j, 0, keepdims=False)
        return (
            lax.dynamic_update_index_in_dim(forward, ahead, k, 0),
            lax.dynamic_update_index_in_dim(backward, behind, j, 0),
        )

    zeros = (jnp.zeros((n_col, block, width), F32), jnp.zeros((n_row, block, width), F32))
    forward, backward = lax.fori_loop(0, tile_count[0], add_slot, zeros)
    summed = lax.psum_scatter(
        forward.astype(BF16).reshape(n_col * block, width), "col", scatter_dimension=0, tiled=True
    ).astype(F32)
    output = jnp.dot(summed.astype(BF16), weight, preferred_element_type=F32).astype(BF16)
    term = lax.dot_general(
        summed, cotangent.astype(F32), ROWS_ROWS, precision=lax.Precision.HIGHEST
    )
    grad_weight = lax.psum(term, ("row", "col")) * (1.0 / math.sqrt(block * n_row * n_col))
    grad_embeddings = lax.psum_scatter(
        backward.astype(BF16).reshape(n_row * block, width), "row", scatter_dimension=0, tiled=True
    )
    return (output, grad_embeddings, grad_weight)


def solution(mesh):
    n_row, n_col = mesh.shape["row"], mesh.shape["col"]

    def local(embeddings, cotangent, weight, tiles, tile_dst, tile_src, tile_count):
        fits = n_row * n_col <= tiles.shape[1] and n_row % 2 == 0
        fits = fits and tiles.shape[1] % CHUNKS == 0 and weight.shape[0] % (16 * n_row) == 0
        body = functools.partial(combined if fits else slotwise, n_row, n_col)
        return body(embeddings, cotangent, weight, tiles, tile_dst, tile_src, tile_count)

    in_specs = (
        P(("row", "col"), None),
        P(("row", "col"), None),
        P(),
        P(("row", "col"), None, None, None),
        P(("row", "col"), None),
        P(("row", "col"), None),
        P(("row", "col")),
    )
    out_specs = (P(("row", "col"), None), P(("row", "col"), None), P())
    return jax.shard_map(local, mesh=mesh, in_specs=in_specs, out_specs=out_specs, check_vma=False)
```

```python
import functools
import math

import jax
import jax.numpy as jnp
from jax import lax
from jax.experimental import pallas as pl
from jax.experimental.pallas import tpu as pltpu
from jax.sharding import PartitionSpec as P

F32 = jnp.float32
BF16 = jnp.bfloat16
ROWS_ROWS = (((0,), (0,)), ((), ()))
COLS_COLS = (((1,), (1,)), ((), ()))
CHUNKS = 4


def fused(
    n_row,
    n_col,
    count_ref,
    dst_ref,
    src_ref,
    emb_ref,
    cot_ref,
    weight_ref,
    tiles_ref,
    out_ref,
    gemb_ref,
    gw_ref,
    link_v,
    link_ref,
    wbuf,
    tbuf,
    chain,
    a_rows,
    a_cols,
    e_all,
    c_all,
    part,
    part_in,
    back_sib,
    back_sib_in,
    back_own,
    back_sum,
    back_in,
    term,
    term_in,
    mid_in,
    fin,
    link_sem,
    own_sem,
    tile_sem,
    e_send,
    e_recv,
    relay_send,
    c_send,
    c_recv,
    p_send,
    p_recv,
    s_send,
    s_recv,
    b_send,
    b_recv,
    t_send,
    t_recv,
    m_send,
    m_recv,
    f_send,
    f_recv,
):
    block, width = emb_ref.shape
    slots = tiles_ref.shape[0]
    n_chip = n_row // 2
    row = lax.axis_index("row")
    col = lax.axis_index("col")
    core = lax.rem(row, 2)
    chip = row // 2
    sibling = row + 1 - 2 * core
    row_peers = [lax.rem(row + i, n_row) for i in range(1, n_row)]
    col_peers = [lax.rem(col + i, n_col) for i in range(1, n_col)]
    chip_peers = [lax.rem(chip + i, n_chip) for i in range(1, n_chip)]

    def remote(src, dst, send, recv, r, c):
        return pltpu.make_async_remote_copy(
            src_ref=src,
            dst_ref=dst,
            send_sem=send,
            recv_sem=recv,
            device_id=(r, c),
            device_id_type=pl.DeviceIdType.MESH,
        )

    sent = []

    def send(*args):
        copy = remote(*args)
        copy.start()
        sent.append(copy)

    def arrived(dst, sems, index):
        remote(dst.at[index], dst.at[index], sems.at[index], sems.at[index], sibling, col).wait_recv()

    barrier = pltpu.get_barrier_semaphore()
    for r in row_peers:
        pl.semaphore_signal(barrier, inc=1, device_id=(r, col), device_id_type=pl.DeviceIdType.MESH)
    for c in col_peers:
        pl.semaphore_signal(barrier, inc=1, device_id=(row, c), device_id_type=pl.DeviceIdType.MESH)

    owned = [(emb_ref, e_all.at[row]), (cot_ref, c_all.at[col]), (weight_ref, wbuf)]
    owned = [pltpu.make_async_copy(a, b, own_sem.at[i]) for i, (a, b) in enumerate(owned)]
    for copy in owned:
        copy.start()
    per = slots // CHUNKS
    loads = []
    for i in range(CHUNKS):
        span = pl.ds(i * per, per)
        load = pltpu.make_async_copy(tiles_ref.at[span], tbuf.at[span], tile_sem.at[i])
        load.start()
        loads.append(load)

    pl.semaphore_wait(barrier, n_row + n_col - 2)

    for p in chip_peers:
        r = 2 * p + core
        send(emb_ref, e_all.at[row], e_send.at[r], e_recv.at[row], r, col)
    for c in col_peers:
        send(cot_ref, c_all.at[col], c_send.at[c], c_recv.at[col], row, c)
    send(emb_ref, e_all.at[row], e_send.at[sibling], e_recv.at[row], sibling, col)

    for copy in owned:
        copy.wait()

    def relay(p):
        r = 2 * p + core
        arrived(e_all, e_recv, r)
        send(e_all.at[r], e_all.at[r], relay_send.at[r], e_recv.at[r], sibling, col)

    spot = lax.broadcasted_iota(jnp.int32, (1, slots), 1)
    code = jnp.where(spot < count_ref[0], dst_ref[...] * n_row + src_ref[...], -1)
    down = jnp.broadcast_to(code, (slots, slots)).T
    ahead = lax.broadcasted_iota(jnp.int32, (slots, slots), 0)
    before = (down == code) & (ahead < lax.broadcasted_iota(jnp.int32, (slots, slots), 1))
    link_v[0:1, :] = jnp.max(jnp.where(before, ahead + 1, 0), axis=0, keepdims=True)
    ends = down == lax.broadcasted_iota(jnp.int32, (slots, slots), 1)
    link_v[1:2, :] = jnp.max(jnp.where(ends, ahead + 1, 0), axis=0, keepdims=True)
    links = pltpu.make_async_copy(link_v, link_ref, link_sem)
    links.start()
    links.wait()

    chain[0] = jnp.zeros((block, block), F32)

    def add_tile(t, carry):
        chain[t + 1] = tbuf[t].astype(F32) + chain[link_ref[0, t]]
        return carry

    for i in range(CHUNKS):
        loads[i].wait()
        lax.fori_loop(i * per, (i + 1) * per, add_tile, 0, unroll=4)
    for p in chip_peers:
        relay(p)

    for k in range(n_col):
        for j in range(n_row):
            tile = chain[link_ref[1, k * n_row + j]].astype(BF16)
            a_rows[k, :, pl.ds(j * block, block)] = tile
            a_cols[j, pl.ds(k * block, block), :] = tile

    arrived(e_all, e_recv, sibling)
    for p in chip_peers:
        arrived(e_all, e_recv, 2 * p + 1 - core)

    sources = e_all[...].reshape(n_row * block, width)
    for k in col_peers + [col]:
        part[k] = jnp.dot(a_rows[k], sources, preferred_element_type=F32).astype(BF16)

    for c in col_peers:
        arrived(c_all, c_recv, c)
    cot_group = c_all[...].reshape(n_col * block, width)
    own_term = lax.dot_general(
        part[...].reshape(n_col * block, width), cot_group, ROWS_ROWS, preferred_element_type=F32
    )
    term[...] = own_term.astype(BF16).reshape(term.shape)
    for r in row_peers:
        send(term.at[r], term_in.at[row], t_send.at[r], t_recv.at[row], r, col)

    for k in col_peers[:2]:
        send(part.at[k], part_in.at[col], p_send.at[k], p_recv.at[col], row, k)

    grad_hidden = lax.dot_general(
        cot_group, wbuf[...], COLS_COLS, preferred_element_type=F32
    ).astype(BF16)

    def back(j):
        return lax.dot_general(a_cols[j], grad_hidden, ROWS_ROWS, preferred_element_type=F32)

    for p in chip_peers + [chip]:
        back_sib[p] = back(2 * p + 1 - core).astype(BF16)
        send(back_sib.at[p], back_sib_in.at[p], s_send.at[p], s_recv.at[p], sibling, col)
    row_sum = term[row].astype(F32)
    for r in row_peers:
        arrived(term_in, t_recv, r)
        row_sum = row_sum + term_in[r].astype(F32)
    mid_in[col] = row_sum.astype(BF16)
    for c in col_peers:
        send(mid_in.at[col], mid_in.at[col], m_send.at[c], m_recv.at[col], row, c)

    for k in col_peers[2:]:
        send(part.at[k], part_in.at[col], p_send.at[k], p_recv.at[col], row, k)

    for p in chip_peers + [chip]:
        back_own[p] = back(2 * p + core)

    for p in chip_peers:
        arrived(back_sib_in, s_recv, p)
        back_sum[p] = (back_own[p] + back_sib_in[p].astype(F32)).astype(BF16)
        send(back_sum.at[p], back_in.at[chip], b_send.at[p], b_recv.at[chip], 2 * p + core, col)

    for c in col_peers:
        arrived(mid_in, m_recv, c)
    whole = mid_in[0].astype(F32)
    for c in range(1, n_col):
        whole = whole + mid_in[c].astype(F32)
    fin[row] = whole.astype(BF16)
    for r in row_peers:
        send(fin.at[row], fin.at[row], f_send.at[r], f_recv.at[row], r, col)

    total = part[col].astype(F32)
    for c in col_peers:
        arrived(part_in, p_recv, c)
        total = total + part_in[c].astype(F32)
    out_ref[...] = jnp.dot(
        total.astype(BF16), wbuf[...], preferred_element_type=F32
    ).astype(BF16)

    arrived(back_sib_in, s_recv, chip)
    grad = back_own[chip] + back_sib_in[chip].astype(F32)
    for p in chip_peers:
        arrived(back_in, b_recv, p)
        grad = grad + back_in[p].astype(F32)
    gemb_ref[...] = grad.astype(BF16)

    for r in row_peers:
        arrived(fin, f_recv, r)
    scale = 1.0 / math.sqrt(block * n_row * n_col)
    gw_ref[...] = fin[...].reshape(gw_ref.shape).astype(F32) * scale

    for copy in sent:
        copy.wait_send()


def hand_over(*refs):
    read, write = refs[-2:]
    reads = [pltpu.make_async_copy(refs[i], refs[i + 6], read.at[i]) for i in range(3)]
    writes = [pltpu.make_async_copy(refs[i + 6], refs[i + 3], write.at[i]) for i in range(3)]
    for copy in reads:
        copy.start()
    for i in range(3):
        reads[i].wait()
        writes[i].start()
    for copy in writes:
        copy.wait()


def combined(n_row, n_col, embeddings, cotangent, weight, tiles, tile_dst, tile_src, tile_count):
    block, width = embeddings.shape
    slots = tiles.shape[1]
    pairs = n_row * n_col
    n_chip = n_row // 2
    strip = weight.shape[0] // n_row
    vmem = pl.BlockSpec(memory_space=pltpu.VMEM)
    whole = pl.BlockSpec(memory_space=pl.ANY)
    dma = pltpu.SemaphoreType.DMA
    results = pl.pallas_call(
        functools.partial(fused, n_row, n_col),
        out_shape=(
            jax.ShapeDtypeStruct((block, width), BF16),
            jax.ShapeDtypeStruct((block, width), BF16),
            jax.ShapeDtypeStruct(weight.shape, F32),
        ),
        in_specs=[
            pl.BlockSpec(memory_space=pltpu.SMEM),
            vmem,
            vmem,
            whole,
            whole,
            whole,
            whole,
        ],
        out_specs=(vmem, vmem, vmem),
        scratch_shapes=[
            pltpu.VMEM((2, slots), jnp.int32),
            pltpu.SMEM((2, slots), jnp.int32),
            pltpu.VMEM(weight.shape, BF16),
            pltpu.VMEM((slots, block, block), BF16),
            pltpu.VMEM((slots + 1, block, block), F32),
            pltpu.VMEM((n_col, block, n_row * block), BF16),
            pltpu.VMEM((n_row, n_col * block, block), BF16),
            pltpu.VMEM((n_row, block, width), BF16),
            pltpu.VMEM((n_col, block, width), BF16),
            pltpu.VMEM((n_col, block, width), BF16),
            pltpu.VMEM((n_col, block, width), BF16),
            pltpu.VMEM((n_chip, block, width), BF16),
            pltpu.VMEM((n_chip, block, width), BF16),
            pltpu.VMEM((n_chip, block, width), F32),
            pltpu.VMEM((n_chip, block, width), BF16),
            pltpu.VMEM((n_chip, block, width), BF16),
            pltpu.VMEM((n_row, strip, width), BF16),
            pltpu.VMEM((n_row, strip, width), BF16),
            pltpu.VMEM((n_col, strip, width), BF16),
            pltpu.VMEM((n_row, strip, width), BF16),
            dma,
            dma((3,)),
            dma((CHUNKS,)),
            dma((n_row,)),
            dma((n_row,)),
            dma((n_row,)),
            dma((n_col,)),
            dma((n_col,)),
            dma((n_col,)),
            dma((n_col,)),
            dma((n_chip,)),
            dma((n_chip,)),
            dma((n_chip,)),
            dma((n_chip,)),
            dma((n_row,)),
            dma((n_row,)),
            dma((n_col,)),
            dma((n_col,)),
            dma((n_row,)),
            dma((n_row,)),
        ],
        compiler_params=pltpu.CompilerParams(
            collective_id=0, has_side_effects=True, vmem_limit_bytes=60 * 1024 * 1024
        ),
    )(tile_count, tile_dst, tile_src, embeddings, cotangent, weight, tiles[0])
    return pl.pallas_call(
        hand_over,
        out_shape=tuple(jax.ShapeDtypeStruct(x.shape, x.dtype) for x in results),
        in_specs=[whole] * 3,
        out_specs=(whole,) * 3,
        scratch_shapes=[pltpu.VMEM(x.shape, x.dtype) for x in results] + [dma((3,)), dma((3,))],
    )(*results)


def slotwise(n_row, n_col, embeddings, cotangent, weight, tiles, tile_dst, tile_src, tile_count):
    block, width = embeddings.shape
    gathered = lax.all_gather(embeddings, "row", axis=0)
    grad_hidden = lax.dot_general(
        cotangent, weight, COLS_COLS, preferred_element_type=F32
    ).astype(BF16)
    grad_group = lax.all_gather(grad_hidden, "col", axis=0)

    def add_slot(t, sums):
        forward, backward = sums
        k, j = tile_dst[0, t], tile_src[0, t]
        tile = lax.dynamic_index_in_dim(tiles[0], t, 0, keepdims=False)
        source = lax.dynamic_index_in_dim(gathered, j, 0, keepdims=False)
        grad = lax.dynamic_index_in_dim(grad_group, k, 0, keepdims=False)
        ahead = jnp.dot(tile, source, preferred_element_type=F32)
        behind = lax.dot_general(tile, grad, ROWS_ROWS, preferred_element_type=F32)
        ahead = ahead + lax.dynamic_index_in_dim(forward, k, 0, keepdims=False)
        behind = behind + lax.dynamic_index_in_dim(backward, j, 0, keepdims=False)
        return (
            lax.dynamic_update_index_in_dim(forward, ahead, k, 0),
            lax.dynamic_update_index_in_dim(backward, behind, j, 0),
        )

    zeros = (jnp.zeros((n_col, block, width), F32), jnp.zeros((n_row, block, width), F32))
    forward, backward = lax.fori_loop(0, tile_count[0], add_slot, zeros)
    summed = lax.psum_scatter(
        forward.astype(BF16).reshape(n_col * block, width), "col", scatter_dimension=0, tiled=True
    ).astype(F32)
    output = jnp.dot(summed.astype(BF16), weight, preferred_element_type=F32).astype(BF16)
    term = lax.dot_general(
        summed, cotangent.astype(F32), ROWS_ROWS, precision=lax.Precision.HIGHEST
    )
    grad_weight = lax.psum(term, ("row", "col")) * (1.0 / math.sqrt(block * n_row * n_col))
    grad_embeddings = lax.psum_scatter(
        backward.astype(BF16).reshape(n_row * block, width), "row", scatter_dimension=0, tiled=True
    )
    return (output, grad_embeddings, grad_weight)


def solution(mesh):
    n_row, n_col = mesh.shape["row"], mesh.shape["col"]

    def local(embeddings, cotangent, weight, tiles, tile_dst, tile_src, tile_count):
        fits = n_row * n_col <= tiles.shape[1] and n_row % 2 == 0
        fits = fits and tiles.shape[1] % CHUNKS == 0 and weight.shape[0] % (16 * n_row) == 0
        body = functools.partial(combined if fits else slotwise, n_row, n_col)
        return body(embeddings, cotangent, weight, tiles, tile_dst, tile_src, tile_count)

    in_specs = (
        P(("row", "col"), None),
        P(("row", "col"), None),
        P(),
        P(("row", "col"), None, None, None),
        P(("row", "col"), None),
        P(("row", "col"), None),
        P(("row", "col")),
    )
    out_specs = (P(("row", "col"), None), P(("row", "col"), None), P())
    return jax.shard_map(local, mesh=mesh, in_specs=in_specs, out_specs=out_specs, check_vma=False)
```
